32 devices in a mesh: groups: 2 (over x), dp: 2 (over core), loop: 8 (over z, y).
Axes of the slice: x: 2, y: 2, z: 4, core: 2. Of those that a mesh axis runs over, the one named last changes fastest.
Arguments:
- tokens: bfloat16 [512, 2304], P(('groups', 'dp', 'loop')), parts along dimension 0, may hold values from -6 to 6
- grad_out: bfloat16 [512, 2304], P(('groups', 'dp', 'loop')), parts along dimension 0, may hold values from -6 to 6
- gate_weight: bfloat16 [2304, 18432], P('dp', 'loop'), may hold values from -0.125 to 0.125
- up_weight: bfloat16 [2304, 18432], P('dp', 'loop'), may hold values from -0.125 to 0.125
- down_weight: bfloat16 [18432, 2304], P('loop', 'dp'), may hold values from -0.046875 to 0.046875
Outputs:
- grad_tokens: bfloat16 [512, 2304], P(('groups', 'dp', 'loop')), parts along dimension 0
- grad_gate: float32 [4608, 18432], P(('groups', 'dp'), 'loop'), parts along dimension 0
- grad_up: float32 [4608, 18432], P(('groups', 'dp'), 'loop'), parts along dimension 0
- grad_down: float32 [36864, 2304], P(('groups', 'loop'), 'dp'), parts along dimension 0
The draws below stay inside these ranges and needn't reach their ends.
There are 2 independent parts, one for each index of `groups`. The reference program is written for one: setup_inputs(seed, part) draws one part's arguments, and reference() takes and returns one part's arrays. A program takes and returns all parts, laid end to end along the dimension named above; an argument that names none is the same for every part. Nothing has to cross between parts.
All inputs are finite; a program needn't handle non-finite values.
Results may differ from the reference program's by a relative error of at most 0.005.
Values may be sent and summed in bfloat16 or wider, within the bound.
A program may use at most 256 MiB of HBM per device.

```python
import jax
import jax.numpy as jnp
from jax import lax

D = 2304
FF = 18432
TOKENS = 256


def levels(key, dims, split, low, largest):
    gain = 1.0
    for dim, blocks in split:
        heights = jax.random.uniform(jax.random.fold_in(jax.random.fold_in(key, 6), dim), (blocks,), jnp.float32, low / len(split), largest / len(split))
        gain = gain * jnp.repeat(jnp.exp(heights), dims[dim] // blocks).reshape((-1,) + (1,) * (len(dims) - 1 - dim))
    return gain


def gaussian(rng, shape, spread, bound, cuts=(), held_as=jnp.bfloat16):
    array = spread * jax.random.normal(rng, shape, jnp.float32)
    if cuts:
        array = array * levels(rng, shape, cuts, -0.22, 0.18)
    return jnp.clip(array, -bound, bound).astype(held_as)


def setup_inputs(seed: int = 0, part: int = 0) -> dict:
    arg_keys = jax.random.split(jax.random.key(seed), 6)
    part_keys = jax.random.split(jax.random.fold_in(arg_keys[5], part), 6)
    return {
        "tokens": gaussian(part_keys[0], (TOKENS, D), 1.0, 6.0, ((0, 16),)),
        "grad_out": gaussian(part_keys[1], (TOKENS, D), 1.0, 6.0, ((0, 16),)),
        "gate_weight": gaussian(arg_keys[2], (D, FF), D ** -0.5, 0.125, ((0, 2), (1, 8))),
        "up_weight": gaussian(arg_keys[3], (D, FF), D ** -0.5, 0.125, ((0, 2), (1, 8))),
        "down_weight": gaussian(arg_keys[4], (FF, D), FF ** -0.5, 0.046875, ((0, 8), (1, 2))),
    }


def reference(tokens, grad_out, gate_weight, up_weight, down_weight):
    gate = jnp.dot(tokens, gate_weight, preferred_element_type=jnp.float32)
    up = jnp.dot(tokens, up_weight, preferred_element_type=jnp.float32)
    grad_hidden = lax.dot_general(grad_out, down_weight, (((1,), (1,)), ((), ())), preferred_element_type=jnp.float32)
    sigma = jax.nn.sigmoid(gate)
    hidden = (gate * sigma * up).astype(jnp.bfloat16)
    grad_gate_pre = (grad_hidden * up * (sigma + gate * sigma * (1.0 - sigma))).astype(jnp.bfloat16)
    grad_up_pre = (grad_hidden * gate * sigma).astype(jnp.bfloat16)
    grad_tokens = lax.dot_general(grad_gate_pre, gate_weight, (((1,), (1,)), ((), ())), preferred_element_type=jnp.float32)
    grad_tokens = grad_tokens + lax.dot_general(grad_up_pre, up_weight, (((1,), (1,)), ((), ())), preferred_element_type=jnp.float32)
    grad_gate = lax.dot_general(tokens, grad_gate_pre, (((0,), (0,)), ((), ())), preferred_element_type=jnp.float32)
    grad_up = lax.dot_general(tokens, grad_up_pre, (((0,), (0,)), ((), ())), preferred_element_type=jnp.float32)
    grad_down = lax.dot_general(hidden, grad_out, (((0,), (0,)), ((), ())), preferred_element_type=jnp.float32)
    return grad_tokens.astype(jnp.bfloat16), grad_gate, grad_up, grad_down
```

```python
import jax
import jax.numpy as jnp
from jax import lax
from jax.sharding import PartitionSpec as P


def contract_last(left, right):
    return lax.dot_general(
        left, right, (((1,), (1,)), ((), ())), preferred_element_type=jnp.float32
    )


def contract_first(left, right):
    return lax.dot_general(
        left, right, (((0,), (0,)), ((), ())), preferred_element_type=jnp.float32
    )


def pointwise(gate, up, grad_hidden):
    sigma = jax.nn.sigmoid(gate)
    hidden = (gate * sigma * up).astype(jnp.bfloat16)
    grad_gate_pre = (grad_hidden * up * (sigma + gate * sigma * (1.0 - sigma))).astype(jnp.bfloat16)
    grad_up_pre = (grad_hidden * gate * sigma).astype(jnp.bfloat16)
    return (hidden, grad_gate_pre, grad_up_pre)


def on_device(tokens, grad_out, gate_weight, up_weight, down_weight):
    def halves(rows):
        rows = lax.all_to_all(rows, "dp", split_axis=1, concat_axis=0, tiled=True)
        return lax.all_gather(rows, "loop", axis=0, tiled=True)

    def both(term):
        sent = term.astype(jnp.bfloat16)
        return term + lax.ppermute(sent, "dp", [(0, 1), (1, 0)]).astype(jnp.float32)

    features, upstream = halves(tokens), halves(grad_out)
    gate = both(jnp.dot(features, gate_weight, preferred_element_type=jnp.float32))
    up = both(jnp.dot(features, up_weight, preferred_element_type=jnp.float32))
    grad_hidden = both(contract_last(upstream, down_weight))
    hidden, grad_gate_pre, grad_up_pre = pointwise(gate, up, grad_hidden)
    grad_rows = lax.psum_scatter(
        contract_last(grad_gate_pre, gate_weight) + contract_last(grad_up_pre, up_weight),
        "loop",
        scatter_dimension=0,
        tiled=True,
    ).astype(jnp.bfloat16)
    grad_tokens = lax.all_to_all(grad_rows, "dp", split_axis=0, concat_axis=1, tiled=True)
    grad_gate = contract_first(features, grad_gate_pre)
    grad_up = contract_first(features, grad_up_pre)
    grad_down = contract_first(hidden, upstream)
    return (grad_tokens, grad_gate, grad_up, grad_down)


def solution(mesh):
    in_specs = (
        P(("groups", "dp", "loop"), None),
        P(("groups", "dp", "loop"), None),
        P("dp", "loop"),
        P("dp", "loop"),
        P("loop", "dp"),
    )
    out_specs = (
        P(("groups", "dp", "loop"), None),
        P(("groups", "dp"), "loop"),
        P(("groups", "dp"), "loop"),
        P(("groups", "loop"), "dp"),
    )
    return jax.shard_map(
        on_device, mesh=mesh, in_specs=in_specs, out_specs=out_specs, check_vma=False
    )
```

```python
import functools

import jax
import jax.numpy as jnp
from jax import lax
from jax.experimental import pallas as pl
from jax.experimental.pallas import tpu as pltpu
from jax.sharding import PartitionSpec as P

MESH = pl.DeviceIdType.MESH
MIB = 1024 * 1024


def contract_last(left, right):
    return lax.dot_general(
        left, right, (((1,), (1,)), ((), ())), preferred_element_type=jnp.float32
    )


def contract_first(left, right):
    return lax.dot_general(
        left, right, (((0,), (0,)), ((), ())), preferred_element_type=jnp.float32
    )


def pointwise(gate, up, grad_hidden):
    sigma = jax.nn.sigmoid(gate)
    hidden = (gate * sigma * up).astype(jnp.bfloat16)
    grad_gate_pre = (grad_hidden * up * (sigma + gate * sigma * (1.0 - sigma))).astype(jnp.bfloat16)
    grad_up_pre = (grad_hidden * gate * sigma).astype(jnp.bfloat16)
    return (hidden, grad_gate_pre, grad_up_pre)


def hidden_kernel(
    loop, width, chunks,
    tokens, grad_out, gate_w, up_w, down_w,
    features, upstream, hidden, grad_gate_pre, grad_up_pre, terms,
    held, gate_v, up_v, down_v, own, sent, got, total,
    load_sem, half_send, half_recv, ring_send, ring_recv, part_send, part_recv,
):
    g, c, l = lax.axis_index("groups"), lax.axis_index("dp"), lax.axis_index("loop")
    depth = loop // width
    z, y = l // width, l % width
    rows, half = tokens.shape[0], gate_w.shape[0]
    chunk = gate_v.shape[2]
    count = loop * 2 * rows

    def load(k, i):
        cols = pl.ds(i * chunk, chunk)
        source = down_w.at[cols] if k == 2 else (gate_w, up_w)[k].at[:, cols]
        return pltpu.make_async_copy(source, (gate_v, up_v, down_v)[k].at[i], load_sem.at[k, i])

    barrier = pltpu.get_barrier_semaphore()

    def greet(device):
        pl.semaphore_signal(barrier, inc=1, device_id=device, device_id_type=MESH)

    greet((g, 1 - c, l))
    if width == 2:
        greet((g, c, z * width + 1 - y))
    pl.when(z > 0)(lambda: greet((g, c, l - width)))
    pl.when(z < depth - 1)(lambda: greet((g, c, l + width)))
    inner = jnp.where(z > 0, 1, 0) + jnp.where(z < depth - 1, 1, 0)
    for k in range(3):
        for i in range(chunks):
            load(k, i).start()
    pl.semaphore_wait(barrier, (2 if width == 2 else 1) + inner)

    mine = pl.ds(pl.multiple_of(c * rows, rows), rows)
    kept = pl.ds(pl.multiple_of(c * half, 128), half)
    given = pl.ds(pl.multiple_of((1 - c) * half, 128), half)

    def swap(a):
        ref = (tokens, grad_out)[a]
        return pltpu.make_async_remote_copy(
            src_ref=ref.at[:, given], dst_ref=held.at[a, l, mine],
            send_sem=half_send.at[a], recv_sem=half_recv.at[a],
            device_id=(g, 1 - c, l), device_id_type=MESH,
        )

    for a in range(2):
        swap(a).start()
    for a in range(2):
        held[a, l, mine, :] = (tokens, grad_out)[a][:, kept]

    def move(a, block, way):
        target = (l + width, l - width, z * width + 1 - y)[way]
        return pltpu.make_async_remote_copy(
            src_ref=held.at[a, block], dst_ref=held.at[a, block],
            send_sem=ring_send.at[a, block, way], recv_sem=ring_recv.at[a, block],
            device_id=(g, c, target), device_id_type=MESH,
        )

    def sends(a, d, act):
        def from_below():
            block = l - d * width
            if act == "start" and d:
                move(a, block, 0).wait_recv()
            pl.when(z < depth - 1)(lambda: getattr(move(a, block, 0), act)())
            if width == 2:
                getattr(move(a, block, 2), act)()

        def from_above():
            block = l + d * width
            if act == "start" and d:
                move(a, block, 1).wait_recv()
            pl.when(z > 0)(lambda: getattr(move(a, block, 1), act)())
            if width == 2 and d:
                getattr(move(a, block, 2), act)()

        if d == 0:
            if act == "start":
                swap(a).wait_recv()
            from_below()
            from_above()
        else:
            pl.when(z - d >= 0)(from_below)
            pl.when(z + d < depth)(from_above)

    def across(a):
        if width == 2:
            for k in range(depth):
                move(a, k * width + 1 - y, 2).wait_recv()

    sends(0, 0, "start")
    for d in range(1, depth):
        sends(0, d, "start")
        sends(1, d - 1, "start")
    across(0)

    def part(k, i):
        return pltpu.make_async_remote_copy(
            src_ref=sent.at[k, i], dst_ref=got.at[k, i],
            send_sem=part_send.at[k, i], recv_sem=part_recv.at[k, i],
            device_id=(g, 1 - c, l), device_id_type=MESH,
        )

    def forward(k):
        def step(i, carry):
            load(k, i).wait()
            x = held[min(1, k // 2)].reshape(count, half)
            if k == 2:
                term = contract_last(x, down_v[i])
            else:
                term = jnp.dot(x, (gate_v, up_v)[k][i], preferred_element_type=jnp.float32)
            own[k, i] = term
            sent[k, i] = term.astype(jnp.bfloat16)
            part(k, i).start()
            return carry

        lax.fori_loop(0, chunks, step, 0)

    forward(0)
    sends(1, depth - 1, "start")
    forward(1)
    across(1)
    forward(2)
    for a, out in enumerate((features, upstream)):
        out[...] = held[a].reshape(count, half)
    total[...] = jnp.zeros_like(total)

    def back(i, carry):
        whole = []
        for k in range(3):
            part(k, i).wait_recv()
            whole.append(own[k, i] + got[k, i].astype(jnp.float32))
        h, gg, gu = pointwise(*whole)
        cols = pl.ds(pl.multiple_of(i * chunk, chunk), chunk)
        hidden[:, cols] = h
        grad_gate_pre[:, cols] = gg
        grad_up_pre[:, cols] = gu
        total[...] += contract_last(gg, gate_v[i]) + contract_last(gu, up_v[i])
        return carry

    lax.fori_loop(0, chunks, back, 0)
    for k in range(loop):
        to = lax.rem(l + k, loop) * 2
        for e in range(2):
            at = to + (c if e == 0 else 1 - c)
            terms[e, k] = total[pl.ds(pl.multiple_of(at * rows, rows), rows), :].astype(jnp.bfloat16)

    def drain(i, carry):
        for k in range(3):
            part(k, i).wait_send()
        return carry

    lax.fori_loop(0, chunks, drain, 0)
    for a in range(2):
        swap(a).wait_send()
        for d in range(depth):
            sends(a, d, "wait_send")


def find_hidden(loop, width, tokens, grad_out, gate_weight, up_weight, down_weight):
    rows = tokens.shape[0]
    half, units = gate_weight.shape
    count = loop * 2 * rows
    chunk = next((n for n in (384, 256, 128) if units % n == 0), units)
    chunks = units // chunk
    bf16, f32 = jnp.bfloat16, jnp.float32
    vmem, far = pl.BlockSpec(memory_space=pltpu.VMEM), pl.BlockSpec(memory_space=pl.ANY)
    dma = pltpu.SemaphoreType.DMA
    return pl.pallas_call(
        functools.partial(hidden_kernel, loop, width, chunks),
        out_shape=[jax.ShapeDtypeStruct((count, half), bf16)] * 2
        + [jax.ShapeDtypeStruct((count, units), bf16)] * 3
        + [jax.ShapeDtypeStruct((2, loop, rows, half), bf16)],
        in_specs=[vmem, vmem, far, far, far],
        out_specs=[vmem] * 6,
        scratch_shapes=[
            pltpu.VMEM((2, loop, 2 * rows, half), bf16),
            pltpu.VMEM((chunks, half, chunk), bf16),
            pltpu.VMEM((chunks, half, chunk), bf16),
            pltpu.VMEM((chunks, chunk, half), bf16),
            pltpu.VMEM((3, chunks, count, chunk), f32),
            pltpu.VMEM((3, chunks, count, chunk), bf16),
            pltpu.VMEM((3, chunks, count, chunk), bf16),
            pltpu.VMEM((count, half), f32),
            dma((3, chunks)), dma((2,)), dma((2,)),
            dma((2, loop, 3)), dma((2, loop)), dma((3, chunks)), dma((3, chunks)),
        ],
        compiler_params=pltpu.CompilerParams(
            collective_id=0, has_side_effects=True, vmem_limit_bytes=58 * MIB
        ),
        cost_estimate=pl.CostEstimate(
            flops=10 * count * half * units,
            bytes_accessed=6 * half * units + 10 * count * (units + half),
            transcendentals=count * units,
        ),
        name="find_hidden",
    )(tokens, grad_out, gate_weight, up_weight, down_weight)


def gradient_kernel(features, grad_gate_pre, grad_up_pre, hidden, upstream, gate, up, down):
    gate[...] = contract_first(features[...], grad_gate_pre[...])
    up[...] = contract_first(features[...], grad_up_pre[...])
    down[...] = contract_first(hidden[...], upstream[...])


def weight_gradients(features, upstream, hidden, grad_gate_pre, grad_up_pre):
    count, half = features.shape
    units = hidden.shape[1]
    steps = half // 128
    if half % 128 or units % (128 * steps):
        return (
            contract_first(features, grad_gate_pre),
            contract_first(features, grad_up_pre),
            contract_first(hidden, upstream),
        )
    whole = lambda cols: pl.BlockSpec((count, cols), lambda i: (0, 0))
    slab = lambda cols: pl.BlockSpec((count, cols), lambda i: (0, i))
    rows = lambda n, cols: pl.BlockSpec((n, cols), lambda i: (i, 0))
    tall, wide = half // steps, units // steps
    return pl.pallas_call(
        gradient_kernel,
        grid=(steps,),
        out_shape=[jax.ShapeDtypeStruct((half, units), jnp.float32)] * 2
        + [jax.ShapeDtypeStruct((units, half), jnp.float32)],
        in_specs=[slab(tall), whole(units), whole(units), slab(wide), whole(half)],
        out_specs=[rows(tall, units), rows(tall, units), rows(wide, half)],
        compiler_params=pltpu.CompilerParams(vmem_limit_bytes=40 * MIB),
        cost_estimate=pl.CostEstimate(
            flops=6 * count * half * units,
            bytes_accessed=12 * half * units + 2 * count * (3 * units + 2 * half),
            transcendentals=0,
        ),
        name="weight_gradients",
    )(features, grad_gate_pre, grad_up_pre, hidden, upstream)


def sum_terms(loop, terms):
    halves = []
    for e in range(2):
        total = None
        for k in range(loop):
            term = terms[e, k]
            if e or k:
                pairs = [
                    (c * loop + l, (c ^ e) * loop + (l + k) % loop)
                    for c in range(2)
                    for l in range(loop)
                ]
                term = lax.ppermute(term, ("dp", "loop"), pairs)
            term = term.astype(jnp.float32)
            total = term if total is None else total + term
        halves.append(total)
    kept, other = halves
    first = lax.axis_index("dp") == 0
    low, high = jnp.where(first, kept, other), jnp.where(first, other, kept)
    return jnp.concatenate([low, high], axis=1).astype(jnp.bfloat16)


def on_device(loop, width, tokens, grad_out, gate_weight, up_weight, down_weight):
    features, upstream, hidden, grad_gate_pre, grad_up_pre, terms = find_hidden(
        loop, width, tokens, grad_out, gate_weight, up_weight, down_weight
    )
    grad_gate, grad_up, grad_down = weight_gradients(
        features, upstream, hidden, grad_gate_pre, grad_up_pre
    )
    return (sum_terms(loop, terms), grad_gate, grad_up, grad_down)


def columns(mesh):
    line = mesh.devices[0, 0]
    z = [getattr(device, "coords", (0, 0, k // 2))[2] for k, device in enumerate(line)]
    side = sum(n == z[0] for n in z)
    return 2 if side == 2 and len(z) % 2 == 0 else 1


def solution(mesh):
    in_specs = (
        P(("groups", "dp", "loop"), None),
        P(("groups", "dp", "loop"), None),
        P("dp", "loop"),
        P("dp", "loop"),
        P("loop", "dp"),
    )
    out_specs = (
        P(("groups", "dp", "loop"), None),
        P(("groups", "dp"), "loop"),
        P(("groups", "dp"), "loop"),
        P(("groups", "loop"), "dp"),
    )
    return jax.shard_map(
        functools.partial(on_device, mesh.shape["loop"], columns(mesh)),
        mesh=mesh, in_specs=in_specs, out_specs=out_specs, check_vma=False,
    )
```

```python
import functools

import jax
import jax.numpy as jnp
from jax import lax
from jax.experimental import pallas as pl
from jax.experimental.pallas import tpu as pltpu
from jax.sharding import PartitionSpec as P

MESH = pl.DeviceIdType.MESH
MIB = 1024 * 1024


def contract_last(left, right):
    return lax.dot_general(
        left, right, (((1,), (1,)), ((), ())), preferred_element_type=jnp.float32
    )


def contract_first(left, right):
    return lax.dot_general(
        left, right, (((0,), (0,)), ((), ())), preferred_element_type=jnp.float32
    )


def pointwise(gate, up, grad_hidden):
    sigma = jax.nn.sigmoid(gate)
    hidden = (gate * sigma * up).astype(jnp.bfloat16)
    grad_gate_pre = (grad_hidden * up * (sigma + gate * sigma * (1.0 - sigma))).astype(jnp.bfloat16)
    grad_up_pre = (grad_hidden * gate * sigma).astype(jnp.bfloat16)
    return (hidden, grad_gate_pre, grad_up_pre)


def hidden_kernel(
    loop, width, chunks, pieces,
    tokens, grad_out, gate_w, up_w, down_w,
    features, upstream, hidden, grad_gate_pre, grad_up_pre, grad_tokens,
    held, gate_v, up_v, down_v, own, sent, got, hidden_v, gate_pre_v, up_pre_v,
    total, y_out, y_in, z_out, z_in, dp_out, final,
    load_sem, half_send, half_recv, ring_send, ring_recv, part_send, part_recv,
    store_sem, y_send, y_recv, z_send, z_recv, dp_send, dp_recv,
):
    g, c, l = lax.axis_index("groups"), lax.axis_index("dp"), lax.axis_index("loop")
    depth = loop // width
    z, y = l // width, l % width
    rows, half = tokens.shape[0], gate_w.shape[0]
    units = gate_w.shape[1]
    chunk, piece = units // chunks, half // pieces
    count = loop * 2 * rows

    def load(k, i):
        cols = pl.ds(pl.multiple_of(i * chunk, chunk), chunk)
        if k == 2:
            source, target = down_w.at[cols], down_v.at[cols]
        else:
            source, target = (gate_w, up_w)[k].at[:, cols], (gate_v, up_v)[k].at[:, cols]
        return pltpu.make_async_copy(source, target, load_sem.at[k, i])

    barrier = pltpu.get_barrier_semaphore()

    def greet(device):
        pl.semaphore_signal(barrier, inc=1, device_id=device, device_id_type=MESH)

    greet((g, 1 - c, l))
    if width == 2:
        greet((g, c, z * width + 1 - y))
    for k in range(1, depth):
        greet((g, c, lax.rem(z + k, depth) * width + y))
    for k in range(3):
        for i in range(chunks):
            load(k, i).start()
    pl.semaphore_wait(barrier, (2 if width == 2 else 1) + depth - 1)

    mine = pl.ds(pl.multiple_of(c * rows, rows), rows)
    kept = pl.ds(pl.multiple_of(c * half, 128), half)
    given = pl.ds(pl.multiple_of((1 - c) * half, 128), half)

    def swap(a):
        ref = (tokens, grad_out)[a]
        return pltpu.make_async_remote_copy(
            src_ref=ref.at[:, given], dst_ref=held.at[a, l, mine],
            send_sem=half_send.at[a], recv_sem=half_recv.at[a],
            device_id=(g, 1 - c, l), device_id_type=MESH,
        )

    for a in range(2):
        swap(a).start()
    for a in range(2):
        held[a, l, mine, :] = (tokens, grad_out)[a][:, kept]

    def move(a, block, way):
        target = (l + width, l - width, z * width + 1 - y)[way]
        return pltpu.make_async_remote_copy(
            src_ref=held.at[a, block], dst_ref=held.at[a, block],
            send_sem=ring_send.at[a, block, way], recv_sem=ring_recv.at[a, block],
            device_id=(g, c, target), device_id_type=MESH,
        )

    def sends(a, d, act):
        def from_below():
            block = l - d * width
            if act == "start" and d:
                move(a, block, 0).wait_recv()
            pl.when(z < depth - 1)(lambda: getattr(move(a, block, 0), act)())
            if width == 2:
                getattr(move(a, block, 2), act)()

        def from_above():
            block = l + d * width
            if act == "start" and d:
                move(a, block, 1).wait_recv()
            pl.when(z > 0)(lambda: getattr(move(a, block, 1), act)())
            if width == 2 and d:
                getattr(move(a, block, 2), act)()

        if d == 0:
            if act == "start":
                swap(a).wait_recv()
            from_below()
            from_above()
        else:
            pl.when(z - d >= 0)(from_below)
            pl.when(z + d < depth)(from_above)

    def across(a):
        if width == 2:
            for k in range(depth):
                move(a, k * width + 1 - y, 2).wait_recv()

    sends(0, 0, "start")
    for d in range(1, depth):
        sends(0, d, "start")
        sends(1, d - 1, "start")
    across(0)

    def part(k, i):
        return pltpu.make_async_remote_copy(
            src_ref=sent.at[k, i], dst_ref=got.at[k, i],
            send_sem=part_send.at[k, i], recv_sem=part_recv.at[k, i],
            device_id=(g, 1 - c, l), device_id_type=MESH,
        )

    def forward(k):
        def step(i, carry):
            load(k, i).wait()
            x = held[min(1, k // 2)].reshape(count, half)
            cols = pl.ds(pl.multiple_of(i * chunk, chunk), chunk)
            if k == 2:
                term = contract_last(x, down_v[cols, :])
            else:
                weight = (gate_v, up_v)[k][:, cols]
                term = jnp.dot(x, weight, preferred_element_type=jnp.float32)
            own[k, i] = term
            sent[k, i] = term.astype(jnp.bfloat16)
            part(k, i).start()
            return carry

        lax.fori_loop(0, chunks, step, 0)

    forward(0)
    sends(1, depth - 1, "start")
    forward(1)
    across(1)
    forward(2)

    def back(i, carry):
        whole = []
        for k in range(3):
            part(k, i).wait_recv()
            whole.append(own[k, i] + got[k, i].astype(jnp.float32))
        cols = pl.ds(pl.multiple_of(i * chunk, chunk), chunk)
        hidden_v[:, cols], gate_pre_v[:, cols], up_pre_v[:, cols] = pointwise(*whole)
        return carry

    lax.fori_loop(0, chunks, back, 0)
    stores = [
        pltpu.make_async_copy(source, target, store_sem.at[k])
        for k, (source, target) in enumerate((
            (held.at[0], features), (held.at[1], upstream),
            (hidden_v, hidden), (gate_pre_v, grad_gate_pre), (up_pre_v, grad_up_pre),
        ))
    ]
    for store in stores:
        store.start()

    def block_rows(level, side):
        return pl.ds(pl.multiple_of((level * width + side) * 2 * rows, 2 * rows), 2 * rows)

    def over_y(p):
        return pltpu.make_async_remote_copy(
            src_ref=y_out.at[p], dst_ref=y_in.at[p],
            send_sem=y_send.at[p], recv_sem=y_recv.at[p],
            device_id=(g, c, z * width + 1 - y), device_id_type=MESH,
        )

    def over_z(p, k):
        return pltpu.make_async_remote_copy(
            src_ref=z_out.at[p, k], dst_ref=z_in.at[p, k],
            send_sem=z_send.at[p, k], recv_sem=z_recv.at[p, k],
            device_id=(g, c, lax.rem(z + k, depth) * width + y), device_id_type=MESH,
        )

    def over_dp(p):
        cols = pl.ds(pl.multiple_of(c * half + p * piece, 128), piece)
        return pltpu.make_async_remote_copy(
            src_ref=dp_out.at[p], dst_ref=final.at[:, cols],
            send_sem=dp_send.at[p], recv_sem=dp_recv.at[p],
            device_id=(g, 1 - c, l), device_id_type=MESH,
        )

    for p in range(pieces):
        part_rows = pl.ds(p * piece, piece)
        total[p] = contract_last(gate_pre_v[...], gate_v[part_rows, :])
        total[p] += contract_last(up_pre_v[...], up_v[part_rows, :])
        if width == 2:
            for k in range(depth):
                y_out[p, k] = total[p, block_rows(k, 1 - y), :].astype(jnp.bfloat16)
            over_y(p).start()
    for p in range(pieces):
        if width == 2:
            over_y(p).wait_recv()
        for k in list(range(1, depth)) + [0]:
            to = lax.rem(z + k, depth)
            term = total[p, block_rows(to, y), :]
            if width == 2:
                term += y_in[p, to].astype(jnp.float32)
            if k:
                z_out[p, k] = term.astype(jnp.bfloat16)
                over_z(p, k).start()
            else:
                total[p, block_rows(z, y), :] = term
    for p in range(pieces):
        for k in range(1, depth):
            over_z(p, k).wait_recv()
        for e in range(2):
            side = c if e else 1 - c
            start = pl.multiple_of((l * 2 + side) * rows, rows)
            term = total[p, pl.ds(start, rows), :]
            for k in range(1, depth):
                term += z_in[p, k, pl.ds(pl.multiple_of(side * rows, rows), rows), :].astype(jnp.float32)
            if e:
                cols = pl.ds(pl.multiple_of(c * half + p * piece, 128), piece)
                final[:, cols] = term.astype(jnp.bfloat16)
            else:
                dp_out[p] = term.astype(jnp.bfloat16)
                over_dp(p).start()
    for p in range(pieces):
        over_dp(p).wait_recv()
    grad_tokens[...] = final[...]

    def drain(i, carry):
        for k in range(3):
            part(k, i).wait_send()
        return carry

    lax.fori_loop(0, chunks, drain, 0)
    for a in range(2):
        swap(a).wait_send()
        for d in range(depth):
            sends(a, d, "wait_send")
    for p in range(pieces):
        if width == 2:
            over_y(p).wait_send()
        for k in range(1, depth):
            over_z(p, k).wait_send()
        over_dp(p).wait_send()
    for store in stores:
        store.wait()


def find_hidden(loop, width, tokens, grad_out, gate_weight, up_weight, down_weight):
    rows = tokens.shape[0]
    half, units = gate_weight.shape
    count, depth = loop * 2 * rows, loop // width
    chunk = next((n for n in (384, 256, 128) if units % n == 0), units)
    piece = next((n for n in (384, 256, 128) if half % n == 0), half)
    chunks, pieces = units // chunk, half // piece
    bf16, f32 = jnp.bfloat16, jnp.float32
    vmem, far = pl.BlockSpec(memory_space=pltpu.VMEM), pl.BlockSpec(memory_space=pl.ANY)
    dma = pltpu.SemaphoreType.DMA
    return pl.pallas_call(
        functools.partial(hidden_kernel, loop, width, chunks, pieces),
        out_shape=[jax.ShapeDtypeStruct((loop, 2 * rows, half), bf16)] * 2
        + [jax.ShapeDtypeStruct((count, units), bf16)] * 3
        + [jax.ShapeDtypeStruct((rows, 2 * half), bf16)],
        in_specs=[vmem, vmem, far, far, far],
        out_specs=[far] * 5 + [vmem],
        scratch_shapes=[
            pltpu.VMEM((2, loop, 2 * rows, half), bf16),
            pltpu.VMEM((half, units), bf16),
            pltpu.VMEM((half, units), bf16),
            pltpu.VMEM((units, half), bf16),
            pltpu.VMEM((3, chunks, count, chunk), f32),
            pltpu.VMEM((3, chunks, count, chunk), bf16),
            pltpu.VMEM((3, chunks, count, chunk), bf16),
            pltpu.VMEM((count, units), bf16),
            pltpu.VMEM((count, units), bf16),
            pltpu.VMEM((count, units), bf16),
            pltpu.VMEM((pieces, count, piece), f32),
            pltpu.VMEM((pieces, depth, 2 * rows, piece), bf16),
            pltpu.VMEM((pieces, depth, 2 * rows, piece), bf16),
            pltpu.VMEM((pieces, depth, 2 * rows, piece), bf16),
            pltpu.VMEM((pieces, depth, 2 * rows, piece), bf16),
            pltpu.VMEM((pieces, rows, piece), bf16),
            pltpu.VMEM((rows, 2 * half), bf16),
            dma((3, chunks)), dma((2,)), dma((2,)),
            dma((2, loop, 3)), dma((2, loop)), dma((3, chunks)), dma((3, chunks)),
            dma((5,)), dma((pieces,)), dma((pieces,)),
            dma((pieces, depth)), dma((pieces, depth)), dma((pieces,)), dma((pieces,)),
        ],
        compiler_params=pltpu.CompilerParams(
            collective_id=0, has_side_effects=True, vmem_limit_bytes=58 * MIB
        ),
        cost_estimate=pl.CostEstimate(
            flops=10 * count * half * units,
            bytes_accessed=6 * half * units + 10 * count * (units + half),
            transcendentals=count * units,
        ),
        name="find_hidden",
    )(tokens, grad_out, gate_weight, up_weight, down_weight)


def gradient_kernel(features, grad_gate_pre, grad_up_pre, hidden, upstream, gate, up, down):
    gate[...] = contract_first(features[...], grad_gate_pre[...])
    up[...] = contract_first(features[...], grad_up_pre[...])
    down[...] = contract_first(hidden[...], upstream[...])


def weight_gradients(features, upstream, hidden, grad_gate_pre, grad_up_pre):
    count, half = features.shape
    units = hidden.shape[1]
    steps = half // 128
    if half % 128 or units % (128 * steps):
        return (
            contract_first(features, grad_gate_pre),
            contract_first(features, grad_up_pre),
            contract_first(hidden, upstream),
        )
    whole = lambda cols: pl.BlockSpec((count, cols), lambda i: (0, 0))
    slab = lambda cols: pl.BlockSpec((count, cols), lambda i: (0, i))
    rows = lambda n, cols: pl.BlockSpec((n, cols), lambda i: (i, 0))
    tall, wide = half // steps, units // steps
    return pl.pallas_call(
        gradient_kernel,
        grid=(steps,),
        out_shape=[jax.ShapeDtypeStruct((half, units), jnp.float32)] * 2
        + [jax.ShapeDtypeStruct((units, half), jnp.float32)],
        in_specs=[slab(tall), whole(units), whole(units), slab(wide), whole(half)],
        out_specs=[rows(tall, units), rows(tall, units), rows(wide, half)],
        compiler_params=pltpu.CompilerParams(vmem_limit_bytes=40 * MIB),
        cost_estimate=pl.CostEstimate(
            flops=6 * count * half * units,
            bytes_accessed=12 * half * units + 2 * count * (3 * units + 2 * half),
            transcendentals=0,
        ),
        name="weight_gradients",
    )(features, grad_gate_pre, grad_up_pre, hidden, upstream)


def on_device(loop, width, tokens, grad_out, gate_weight, up_weight, down_weight):
    features, upstream, hidden, grad_gate_pre, grad_up_pre, grad_tokens = find_hidden(
        loop, width, tokens, grad_out, gate_weight, up_weight, down_weight
    )
    features, upstream = (x.reshape(-1, x.shape[2]) for x in (features, upstream))
    grad_gate, grad_up, grad_down = weight_gradients(
        features, upstream, hidden, grad_gate_pre, grad_up_pre
    )
    return (grad_tokens, grad_gate, grad_up, grad_down)


def columns(mesh):
    line = mesh.devices[0, 0]
    z = [getattr(device, "coords", (0, 0, k // 2))[2] for k, device in enumerate(line)]
    side = sum(n == z[0] for n in z)
    return 2 if side == 2 and len(z) % 2 == 0 else 1


def solution(mesh):
    in_specs = (
        P(("groups", "dp", "loop"), None),
        P(("groups", "dp", "loop"), None),
        P("dp", "loop"),
        P("dp", "loop"),
        P("loop", "dp"),
    )
    out_specs = (
        P(("groups", "dp", "loop"), None),
        P(("groups", "dp"), "loop"),
        P(("groups", "dp"), "loop"),
        P(("groups", "loop"), "dp"),
    )
    return jax.shard_map(
        functools.partial(on_device, mesh.shape["loop"], columns(mesh)),
        mesh=mesh, in_specs=in_specs, out_specs=out_specs, check_vma=False,
    )
```

```python
import functools

import jax
import jax.numpy as jnp
from jax import lax
from jax.experimental import pallas as pl
from jax.experimental.pallas import tpu as pltpu
from jax.sharding import PartitionSpec as P

MESH = pl.DeviceIdType.MESH
MIB = 1024 * 1024


def contract_last(left, right):
    return lax.dot_general(
        left, right, (((1,), (1,)), ((), ())), preferred_element_type=jnp.float32
    )


def contract_first(left, right):
    return lax.dot_general(
        left, right, (((0,), (0,)), ((), ())), preferred_element_type=jnp.float32
    )


def pointwise(gate, up, grad_hidden):
    sigma = jax.nn.sigmoid(gate)
    hidden = (gate * sigma * up).astype(jnp.bfloat16)
    grad_gate_pre = (grad_hidden * up * (sigma + gate * sigma * (1.0 - sigma))).astype(jnp.bfloat16)
    grad_up_pre = (grad_hidden * gate * sigma).astype(jnp.bfloat16)
    return (hidden, grad_gate_pre, grad_up_pre)


def hidden_kernel(
    loop, width, chunks, pieces,
    tokens, grad_out, gate_w, up_w, down_w,
    features, upstream, hidden, grad_gate_pre, grad_up_pre, grad_tokens,
    held, gate_v, up_v, down_v, own, sent, got, hidden_v, gate_pre_v, up_pre_v,
    total, y_out, y_in, z_out, z_in, dp_out, final,
    load_sem, half_send, half_recv, ring_send, ring_recv, part_send, part_recv,
    store_sem, y_send, y_recv, z_send, z_recv, dp_send, dp_recv,
):
    g, c, l = lax.axis_index("groups"), lax.axis_index("dp"), lax.axis_index("loop")
    depth = loop // width
    z, y = l // width, l % width
    rows, half = tokens.shape[0], gate_w.shape[0]
    units = gate_w.shape[1]
    chunk, piece = units // chunks, half // pieces
    count = loop * 2 * rows

    def load(k, i):
        cols = pl.ds(pl.multiple_of(i * chunk, chunk), chunk)
        if k == 2:
            source, target = down_w.at[cols], down_v.at[cols]
        else:
            source, target = (gate_w, up_w)[k].at[:, cols], (gate_v, up_v)[k].at[:, cols]
        return pltpu.make_async_copy(source, target, load_sem.at[k, i])

    barrier = pltpu.get_barrier_semaphore()

    def greet(device):
        pl.semaphore_signal(barrier, inc=1, device_id=device, device_id_type=MESH)

    greet((g, 1 - c, l))
    if width == 2:
        greet((g, c, z * width + 1 - y))
    for k in range(1, depth):
        greet((g, c, lax.rem(z + k, depth) * width + y))
    pl.semaphore_wait(barrier, (2 if width == 2 else 1) + depth - 1)

    mine = pl.ds(pl.multiple_of(c * rows, rows), rows)
    kept = pl.ds(pl.multiple_of(c * half, 128), half)
    given = pl.ds(pl.multiple_of((1 - c) * half, 128), half)

    def swap(a):
        ref = (tokens, grad_out)[a]
        return pltpu.make_async_remote_copy(
            src_ref=ref.at[:, given], dst_ref=held.at[a, l, mine],
            send_sem=half_send.at[a], recv_sem=half_recv.at[a],
            device_id=(g, 1 - c, l), device_id_type=MESH,
        )

    for a in range(2):
        swap(a).start()
    for a in range(2):
        held[a, l, mine, :] = (tokens, grad_out)[a][:, kept]

    def move(a, block, way):
        target = (l + width, l - width, z * width + 1 - y)[way]
        return pltpu.make_async_remote_copy(
            src_ref=held.at[a, block], dst_ref=held.at[a, block],
            send_sem=ring_send.at[a, block, way], recv_sem=ring_recv.at[a, block],
            device_id=(g, c, target), device_id_type=MESH,
        )

    def sends(a, d, act):
        def from_below():
            block = l - d * width
            if act == "start" and d:
                move(a, block, 0).wait_recv()
            pl.when(z < depth - 1)(lambda: getattr(move(a, block, 0), act)())
            if width == 2:
                getattr(move(a, block, 2), act)()

        def from_above():
            block = l + d * width
            if act == "start" and d:
                move(a, block, 1).wait_recv()
            pl.when(z > 0)(lambda: getattr(move(a, block, 1), act)())
            if width == 2 and d:
                getattr(move(a, block, 2), act)()

        if d == 0:
            if act == "start":
                swap(a).wait_recv()
            from_below()
            from_above()
        else:
            pl.when(z - d >= 0)(from_below)
            pl.when(z + d < depth)(from_above)

    def across(a):
        if width == 2:
            for k in range(depth):
                move(a, k * width + 1 - y, 2).wait_recv()

    sends(0, 0, "start")
    sends(1, 0, "start")
    sends(0, 1, "start")
    sends(1, 1, "start")
    for k in range(3):
        for i in range(chunks):
            load(k, i).start()
    for d in range(2, depth):
        sends(0, d, "start")
        if d < depth - 1:
            sends(1, d, "start")
    across(0)

    def part(k, i):
        return pltpu.make_async_remote_copy(
            src_ref=sent.at[k, i], dst_ref=got.at[k, i],
            send_sem=part_send.at[k, i], recv_sem=part_recv.at[k, i],
            device_id=(g, 1 - c, l), device_id_type=MESH,
        )

    def forward(k):
        def step(i, carry):
            load(k, i).wait()
            x = held[min(1, k // 2)].reshape(count, half)
            cols = pl.ds(pl.multiple_of(i * chunk, chunk), chunk)
            if k == 2:
                term = contract_last(x, down_v[cols, :])
            else:
                weight = (gate_v, up_v)[k][:, cols]
                term = jnp.dot(x, weight, preferred_element_type=jnp.float32)
            own[k, i] = term
            sent[k, i] = term.astype(jnp.bfloat16)
            part(k, i).start()
            return carry

        lax.fori_loop(0, chunks, step, 0)

    forward(0)
    sends(1, depth - 1, "start")
    forward(1)
    across(1)
    forward(2)

    def back(i, carry):
        whole = []
        for k in range(3):
            part(k, i).wait_recv()
            whole.append(own[k, i] + got[k, i].astype(jnp.float32))
        cols = pl.ds(pl.multiple_of(i * chunk, chunk), chunk)
        hidden_v[:, cols], gate_pre_v[:, cols], up_pre_v[:, cols] = pointwise(*whole)
        return carry

    lax.fori_loop(0, chunks, back, 0)
    stores = [
        pltpu.make_async_copy(source, target, store_sem.at[k])
        for k, (source, target) in enumerate((
            (held.at[0], features), (held.at[1], upstream),
            (hidden_v, hidden), (gate_pre_v, grad_gate_pre), (up_pre_v, grad_up_pre),
        ))
    ]
    for store in stores:
        store.start()

    def block_rows(level, side):
        return pl.ds(pl.multiple_of((level * width + side) * 2 * rows, 2 * rows), 2 * rows)

    def over_y(p):
        return pltpu.make_async_remote_copy(
            src_ref=y_out.at[p], dst_ref=y_in.at[p],
            send_sem=y_send.at[p], recv_sem=y_recv.at[p],
            device_id=(g, c, z * width + 1 - y), device_id_type=MESH,
        )

    def over_z(p, k):
        return pltpu.make_async_remote_copy(
            src_ref=z_out.at[p, k], dst_ref=z_in.at[p, k],
            send_sem=z_send.at[p, k], recv_sem=z_recv.at[p, k],
            device_id=(g, c, lax.rem(z + k, depth) * width + y), device_id_type=MESH,
        )

    def over_dp(p):
        cols = pl.ds(pl.multiple_of(c * half + p * piece, 128), piece)
        return pltpu.make_async_remote_copy(
            src_ref=dp_out.at[p], dst_ref=final.at[:, cols],
            send_sem=dp_send.at[p], recv_sem=dp_recv.at[p],
            device_id=(g, 1 - c, l), device_id_type=MESH,
        )

    for p in range(pieces):
        part_rows = pl.ds(p * piece, piece)
        total[p] = contract_last(gate_pre_v[...], gate_v[part_rows, :])
        total[p] += contract_last(up_pre_v[...], up_v[part_rows, :])
        if width == 2:
            for k in range(depth):
                y_out[p, k] = total[p, block_rows(k, 1 - y), :].astype(jnp.bfloat16)
            over_y(p).start()
    for p in range(pieces):
        if width == 2:
            over_y(p).wait_recv()
        for k in list(range(1, depth)) + [0]:
            to = lax.rem(z + k, depth)
            term = total[p, block_rows(to, y), :]
            if width == 2:
                term += y_in[p, to].astype(jnp.float32)
            if k:
                z_out[p, k] = term.astype(jnp.bfloat16)
                over_z(p, k).start()
            else:
                total[p, block_rows(z, y), :] = term
    for p in range(pieces):
        for k in range(1, depth):
            over_z(p, k).wait_recv()
        for e in range(2):
            side = c if e else 1 - c
            start = pl.multiple_of((l * 2 + side) * rows, rows)
            term = total[p, pl.ds(start, rows), :]
            for k in range(1, depth):
                term += z_in[p, k, pl.ds(pl.multiple_of(side * rows, rows), rows), :].astype(jnp.float32)
            if e:
                cols = pl.ds(pl.multiple_of(c * half + p * piece, 128), piece)
                final[:, cols] = term.astype(jnp.bfloat16)
            else:
                dp_out[p] = term.astype(jnp.bfloat16)
                over_dp(p).start()
    for p in range(pieces):
        over_dp(p).wait_recv()
    grad_tokens[...] = final[...]

    def drain(i, carry):
        for k in range(3):
            part(k, i).wait_send()
        return carry

    lax.fori_loop(0, chunks, drain, 0)
    for a in range(2):
        swap(a).wait_send()
        for d in range(depth):
            sends(a, d, "wait_send")
    for p in range(pieces):
        if width == 2:
            over_y(p).wait_send()
        for k in range(1, depth):
            over_z(p, k).wait_send()
        over_dp(p).wait_send()
    for store in stores:
        store.wait()


def find_hidden(loop, width, tokens, grad_out, gate_weight, up_weight, down_weight):
    rows = tokens.shape[0]
    half, units = gate_weight.shape
    count, depth = loop * 2 * rows, loop // width
    chunk = next((n for n in (768, 384, 256, 128) if units % n == 0), units)
    piece = next((n for n in (384, 256, 128) if half % n == 0), half)
    chunks, pieces = units // chunk, half // piece
    bf16, f32 = jnp.bfloat16, jnp.float32
    vmem, far = pl.BlockSpec(memory_space=pltpu.VMEM), pl.BlockSpec(memory_space=pl.ANY)
    dma = pltpu.SemaphoreType.DMA
    return pl.pallas_call(
        functools.partial(hidden_kernel, loop, width, chunks, pieces),
        out_shape=[jax.ShapeDtypeStruct((loop, 2 * rows, half), bf16)] * 2
        + [jax.ShapeDtypeStruct((count, units), bf16)] * 3
        + [jax.ShapeDtypeStruct((rows, 2 * half), bf16)],
        in_specs=[vmem, vmem, far, far, far],
        out_specs=[far] * 5 + [vmem],
        scratch_shapes=[
            pltpu.VMEM((2, loop, 2 * rows, half), bf16),
            pltpu.VMEM((half, units), bf16),
            pltpu.VMEM((half, units), bf16),
            pltpu.VMEM((units, half), bf16),
            pltpu.VMEM((3, chunks, count, chunk), f32),
            pltpu.VMEM((3, chunks, count, chunk), bf16),
            pltpu.VMEM((3, chunks, count, chunk), bf16),
            pltpu.VMEM((count, units), bf16),
            pltpu.VMEM((count, units), bf16),
            pltpu.VMEM((count, units), bf16),
            pltpu.VMEM((pieces, count, piece), f32),
            pltpu.VMEM((pieces, depth, 2 * rows, piece), bf16),
            pltpu.VMEM((pieces, depth, 2 * rows, piece), bf16),
            pltpu.VMEM((pieces, depth, 2 * rows, piece), bf16),
            pltpu.VMEM((pieces, depth, 2 * rows, piece), bf16),
            pltpu.VMEM((pieces, rows, piece), bf16),
            pltpu.VMEM((rows, 2 * half), bf16),
            dma((3, chunks)), dma((2,)), dma((2,)),
            dma((2, loop, 3)), dma((2, loop)), dma((3, chunks)), dma((3, chunks)),
            dma((5,)), dma((pieces,)), dma((pieces,)),
            dma((pieces, depth)), dma((pieces, depth)), dma((pieces,)), dma((pieces,)),
        ],
        compiler_params=pltpu.CompilerParams(
            collective_id=0, has_side_effects=True, vmem_limit_bytes=58 * MIB
        ),
        cost_estimate=pl.CostEstimate(
            flops=10 * count * half * units,
            bytes_accessed=6 * half * units + 10 * count * (units + half),
            transcendentals=count * units,
        ),
        name="find_hidden",
    )(tokens, grad_out, gate_weight, up_weight, down_weight)


def gradient_kernel(features, grad_gate_pre, grad_up_pre, hidden, upstream, gate, up, down):
    gate[...] = contract_first(features[...], grad_gate_pre[...])
    up[...] = contract_first(features[...], grad_up_pre[...])
    down[...] = contract_first(hidden[...], upstream[...])


def weight_gradients(features, upstream, hidden, grad_gate_pre, grad_up_pre):
    count, half = features.shape
    units = hidden.shape[1]
    steps = half // 128
    if half % 128 or units % (128 * steps):
        return (
            contract_first(features, grad_gate_pre),
            contract_first(features, grad_up_pre),
            contract_first(hidden, upstream),
        )
    whole = lambda cols: pl.BlockSpec((count, cols), lambda i: (0, 0))
    slab = lambda cols: pl.BlockSpec((count, cols), lambda i: (0, i))
    rows = lambda n, cols: pl.BlockSpec((n, cols), lambda i: (i, 0))
    tall, wide = half // steps, units // steps
    return pl.pallas_call(
        gradient_kernel,
        grid=(steps,),
        out_shape=[jax.ShapeDtypeStruct((half, units), jnp.float32)] * 2
        + [jax.ShapeDtypeStruct((units, half), jnp.float32)],
        in_specs=[slab(tall), whole(units), whole(units), slab(wide), whole(half)],
        out_specs=[rows(tall, units), rows(tall, units), rows(wide, half)],
        compiler_params=pltpu.CompilerParams(vmem_limit_bytes=58 * MIB),
        cost_estimate=pl.CostEstimate(
            flops=6 * count * half * units,
            bytes_accessed=12 * half * units + 2 * count * (3 * units + 2 * half),
            transcendentals=0,
        ),
        name="weight_gradients",
    )(features, grad_gate_pre, grad_up_pre, hidden, upstream)


def on_device(loop, width, tokens, grad_out, gate_weight, up_weight, down_weight):
    features, upstream, hidden, grad_gate_pre, grad_up_pre, grad_tokens = find_hidden(
        loop, width, tokens, grad_out, gate_weight, up_weight, down_weight
    )
    features, upstream = (x.reshape(-1, x.shape[2]) for x in (features, upstream))
    grad_gate, grad_up, grad_down = weight_gradients(
        features, upstream, hidden, grad_gate_pre, grad_up_pre
    )
    return (grad_tokens, grad_gate, grad_up, grad_down)


def columns(mesh):
    line = mesh.devices[0, 0]
    z = [getattr(device, "coords", (0, 0, k // 2))[2] for k, device in enumerate(line)]
    side = sum(n == z[0] for n in z)
    return 2 if side == 2 and len(z) % 2 == 0 else 1


def solution(mesh):
    in_specs = (
        P(("groups", "dp", "loop"), None),
        P(("groups", "dp", "loop"), None),
        P("dp", "loop"),
        P("dp", "loop"),
        P("loop", "dp"),
    )
    out_specs = (
        P(("groups", "dp", "loop"), None),
        P(("groups", "dp"), "loop"),
        P(("groups", "dp"), "loop"),
        P(("groups", "loop"), "dp"),
    )
    return jax.shard_map(
        functools.partial(on_device, mesh.shape["loop"], columns(mesh)),
        mesh=mesh, in_specs=in_specs, out_specs=out_specs, check_vma=False,
    )
```
